512 devices in a mesh: dom: 64 (over x, z, core), sub: 8 (over y).
Axes of the slice: x: 4, y: 8, z: 8, core: 2. Of those that a mesh axis runs over, the one named last changes fastest.
Arguments:
- a_blocks: bfloat16 [8192, 7, 128, 128], P(('dom', 'sub')), may hold values from -6 to 6
- p_blocks: bfloat16 [8192, 128, 128], P(('dom', 'sub')), may hold values from -0.5 to 0.5
- a_cols: int32 [8192, 7], P(('dom', 'sub')), may hold values from 0 to 8191, as said below
- a_target: int32 [8192, 7], P(('dom', 'sub')), may hold values from 0 to 6
- agg: int32 [8192], P(('dom', 'sub')), may hold values from 0 to 2047, as said below
- refine: int32 [8192], P(('dom', 'sub')), may hold values from 0 to 1, as said below
Outputs:
- coarse_blocks: bfloat16 [2048, 7, 128, 128], P(('dom', 'sub'))
The draws below stay inside these ranges and needn't reach their ends.
Inputs may be any that keep to these rules, and one draw needn't show every extreme that they name: a_cols[i, 0] = i, and every entry lies within 16 of its row index i. Fine row i, the r-th of device d = i // 16, has agg[i] = d * 4 + r // 4, except that one of the first 2 rows of a device may name d * 4 - 1 and one of the last 2 may name (d + 1) * 4. `refine`: at most 8 rows of one device are marked, and some device has exactly 8.
All inputs are finite; a program needn't handle non-finite values.
Results may differ from the reference program's by a relative error of at most 0.0049.
Values may be sent and summed in bfloat16 or wider, within the bound.
No kernel may reach another device: no remote copies, remote signals or barrier semaphores. Data moves between devices by JAX's collectives and lax.ppermute only.
A program may use at most 64 MiB of HBM per device.

```python
import jax
import jax.numpy as jnp
from jax import lax

ROWS_DEV = 16
BLOCK_DIM = 128
SLOTS_FINE = 7
SLOTS_COARSE = 7
ALWAYS_LIVE = 3
AGG_SIZE = 4
EDGE_ROWS = 2
COARSE_DEV = 4
REFINED_MAX = 8
FINE_ROWS = 8192
COARSE_ROWS = 2048


def draw_a_cols(key, part):
    key = jax.random.fold_in(key, 11)
    offsets = jax.random.randint(key, (FINE_ROWS, SLOTS_FINE), -ROWS_DEV, ROWS_DEV + 1)
    row_index = jnp.arange(FINE_ROWS, dtype=jnp.int32)
    columns = jnp.clip(row_index[:, None] + offsets, 0, FINE_ROWS - 1)
    columns = columns.at[:, 0].set(row_index)
    columns = columns.at[ROWS_DEV, 1].set(0)
    columns = columns.at[FINE_ROWS - 1 - ROWS_DEV, 2].set(FINE_ROWS - 1)
    return columns.astype(jnp.int32)


def draw_agg(key, part):
    key = jax.random.fold_in(key, 12)
    pick_key, flip_key = jax.random.split(key, 2)
    device_count = FINE_ROWS // ROWS_DEV
    row_index = jnp.arange(FINE_ROWS, dtype=jnp.int32)
    local = row_index % ROWS_DEV
    device = row_index // ROWS_DEV
    base = device * COARSE_DEV + local // AGG_SIZE
    picks = jax.random.randint(pick_key, (device_count, 2), 0, EDGE_ROWS)
    flips = jax.random.randint(flip_key, (device_count, 2), 0, 2)
    lower = (local == picks[device, 0]) & (device > 0) & (flips[device, 0] == 1)
    upper = (local == ROWS_DEV - 1 - picks[device, 1]) & (device < device_count - 1) & (flips[device, 1] == 1)
    result = jnp.where(lower, device * COARSE_DEV - 1, jnp.where(upper, (device + 1) * COARSE_DEV, base))
    return result.astype(jnp.int32)


def draw_refine(key, part):
    key = jax.random.fold_in(key, 13)
    first_key, second_key, third_key = jax.random.split(key, 3)
    device_count = FINE_ROWS // ROWS_DEV
    center = jax.random.randint(first_key, (), 0, device_count)
    device_ids = jnp.arange(device_count, dtype=jnp.int32)
    band = max(device_count // 8, 1)
    scattered = jnp.minimum(jax.random.randint(second_key, (device_count,), 0, 3), REFINED_MAX)
    counts = jnp.where(jnp.abs(device_ids - center) < band, REFINED_MAX, scattered)
    row_keys = jax.random.split(third_key, device_count)
    ranks = jax.vmap(lambda subkey: jax.random.permutation(subkey, ROWS_DEV))(row_keys)
    return (ranks < counts[:, None]).reshape(-1).astype(jnp.int32)


def place_ends(values, key, least, largest):
    shape = values.shape
    place = [jax.random.randint(jax.random.fold_in(key, axis), (), 0, shape[axis]) for axis in range(len(shape))]
    values = values.at[tuple(place)].set(least)
    longest = shape.index(max(shape))
    place[longest] = (place[longest] + 1) % shape[longest]
    return values.at[tuple(place)].set(largest)


def levels(stream_key, shape, pieces, least, high):
    gain = 1.0
    for axis_at, blocks in pieces:
        heights = jax.random.uniform(jax.random.fold_in(jax.random.fold_in(stream_key, 6), axis_at), (blocks,), jnp.float32, least / len(pieces), high / len(pieces))
        gain = gain * jnp.repeat(jnp.exp(heights), shape[axis_at] // blocks).reshape((-1,) + (1,) * (len(shape) - 1 - axis_at))
    return gain


def noise(stream_key, extent, deviation, limit, cuts=(), held_as=jnp.bfloat16):
    array = jax.random.normal(stream_key, extent, jnp.float32) * deviation
    if len(cuts) > 0:
        array = levels(stream_key, extent, cuts, -0.22, 0.18) * array
    return jnp.clip(array, min=-limit, max=limit).astype(held_as)


def setup_inputs(seed: int = 0) -> dict:
    arg_keys = jax.random.split(jax.random.key(seed), 7)
    a_blocks = noise(arg_keys[0], (FINE_ROWS, SLOTS_FINE, BLOCK_DIM, BLOCK_DIM), 1.0, 6.0, ((0, 512),))
    p_blocks = noise(arg_keys[1], (FINE_ROWS, BLOCK_DIM, BLOCK_DIM), BLOCK_DIM ** -0.5, 0.5, ((0, 512),))
    a_cols = draw_a_cols(jax.random.fold_in(arg_keys[6], 71), 0)
    a_target = place_ends(jax.random.randint(arg_keys[3], (FINE_ROWS, SLOTS_FINE), 0, SLOTS_COARSE), jax.random.fold_in(arg_keys[3], 1), 0, SLOTS_COARSE - 1).astype(jnp.int32)
    agg = draw_agg(jax.random.fold_in(arg_keys[6], 71), 0)
    refine = draw_refine(jax.random.fold_in(arg_keys[6], 71), 0)
    return dict(a_blocks=a_blocks, p_blocks=p_blocks, a_cols=a_cols, a_target=a_target, agg=agg, refine=refine)


def reference(a_blocks, p_blocks, a_cols, a_target, agg, refine):
    fine_count = p_blocks.shape[0]
    block_dim = p_blocks.shape[1]
    step_count = fine_count // ROWS_DEV
    slot_index = jnp.arange(SLOTS_FINE)
    live_all = ((slot_index[None, :] < ALWAYS_LIVE) | (refine[:, None] == 1)).astype(jnp.float32)
    initial = jnp.zeros((COARSE_ROWS * SLOTS_COARSE, block_dim, block_dim), jnp.float32)

    def advance(step, accum):
        start = (step * ROWS_DEV).astype(jnp.int32)
        blocks_here = lax.dynamic_slice_in_dim(a_blocks, start, ROWS_DEV, 0).astype(jnp.float32)
        cols_here = lax.dynamic_slice_in_dim(a_cols, start, ROWS_DEV, 0).astype(jnp.int32)
        target_here = lax.dynamic_slice_in_dim(a_target, start, ROWS_DEV, 0).astype(jnp.int32)
        agg_here = lax.dynamic_slice_in_dim(agg, start, ROWS_DEV, 0).astype(jnp.int32)
        live_here = lax.dynamic_slice_in_dim(live_all, start, ROWS_DEV, 0)
        coupled = p_blocks[cols_here].astype(jnp.float32)
        products = jnp.einsum("rkij,rkjc->rkic", blocks_here, coupled,
                              precision=lax.Precision.HIGHEST).astype(jnp.bfloat16)
        own_rows = lax.dynamic_slice_in_dim(p_blocks, start, ROWS_DEV, 0).astype(jnp.float32)
        terms = jnp.einsum("rfb,rkfc->rkbc", own_rows, products.astype(jnp.float32),
                           precision=lax.Precision.HIGHEST)
        terms = terms * live_here[:, :, None, None]
        segment = (agg_here[:, None] * SLOTS_COARSE + target_here).reshape(-1).astype(jnp.int32)
        return accum.at[segment].add(terms.reshape(-1, block_dim, block_dim))

    accum = lax.fori_loop(0, step_count, advance, initial)
    return accum.reshape(COARSE_ROWS, SLOTS_COARSE, block_dim, block_dim).astype(jnp.bfloat16)
```

```python
import jax
import jax.numpy as jnp
from jax import lax
from jax.experimental import pallas as pl
from jax.experimental.pallas import tpu as pltpu
from jax.sharding import PartitionSpec as P

ROWS = 16
DIM = 128
SLOTS = 7
LIVE = 3
COARSE = 4
SEGS = COARSE * SLOTS
DUMP = SEGS
UNROLL = 8
HALO_MAX = 64 + UNROLL
LIST = 128
MSG = SLOTS * DIM + 16
AXES = ("dom", "sub")
F32 = jnp.float32
BF16 = jnp.bfloat16

SMEM = pl.BlockSpec(memory_space=pltpu.SMEM)
VMEM = pl.BlockSpec(memory_space=pltpu.VMEM)
ANY = pl.BlockSpec(memory_space=pl.ANY)


def dot(x, y):
    return jnp.dot(x, y, preferred_element_type=F32)


def run_copies(copies):
    for copy in copies:
        copy.start()
    for copy in copies:
        copy.wait()


def moved_row(agg, first_row, up):
    first_coarse = first_row // COARSE
    low = agg[0] < first_coarse
    low_any = low | (agg[1] < first_coarse)
    high = agg[ROWS - 1] >= first_coarse + COARSE
    high_any = high | (agg[ROWS - 2] >= first_coarse + COARSE)
    row = jnp.where(up, jnp.where(high, ROWS - 1, ROWS - 2), jnp.where(low, 0, 1))
    return row, jnp.where(up, high_any, low_any)


def edge_kernel(cols, target, agg, refine, a, p, msg_a, msg_b, a_buf, p_buf, sems):
    first_row = cols[0, 0]
    odd = (first_row // ROWS) % 2 == 1
    picks = [moved_row(agg, first_row, odd), moved_row(agg, first_row, jnp.logical_not(odd))]
    copies = []
    for side, (row, _) in enumerate(picks):
        copies.append(pltpu.make_async_copy(p.at[row], p_buf.at[side], sems.at[2 * side]))
        copies.append(pltpu.make_async_copy(a.at[row], a_buf.at[side], sems.at[2 * side + 1]))
    for copy in copies:
        copy.start()
    lane = lax.broadcasted_iota(jnp.int32, (16, DIM), 1)
    for side, (row, found) in enumerate(picks):
        msg = (msg_a, msg_b)[side]
        up = odd if side == 0 else jnp.logical_not(odd)
        shift = jnp.where(up, 2 - ROWS, 2 + ROWS) + ROWS - first_row
        fine = refine[row] == 1
        note = jnp.zeros((16, DIM), F32)
        for k in range(SLOTS):
            live = found if k < LIVE else found & fine
            column = (cols[row, k] + shift).astype(F32)
            aim = jnp.where(live, target[row, k], SLOTS).astype(F32)
            note = jnp.where(lane == 2 * k, column, note)
            note = jnp.where(lane == 2 * k + 1, aim, note)
        msg[SLOTS * DIM : MSG, :] = note.astype(BF16)
    for side in range(2):
        msg = (msg_a, msg_b)[side]
        copies[2 * side].wait()
        copies[2 * side + 1].wait()
        turned = p_buf[side].T
        for k in range(SLOTS):
            msg[k * DIM : (k + 1) * DIM, :] = dot(turned, a_buf[side, k]).astype(BF16)


def add_items(count, codes, left, right, acc, by_slot):
    def step(at, carry):
        parts = []
        for j in range(UNROLL):
            n = at * UNROLL + j
            code = codes[n]
            slot = (code & 127) if by_slot else n
            parts.append((code >> 12, dot(left[slot], right[(code >> 7) & 31])))
        for seg, part in parts:
            acc[seg] += part
        return carry

    lax.fori_loop(0, (count + UNROLL - 1) // UNROLL, step, 0)


def own_kernel(cols, target, agg, refine, a, p, acc, left_halo, halo, halo_count, own, left):
    first_row = cols[0, 0]
    first_coarse = first_row // COARSE

    def listing(row, counts):
        own_n, halo_n = counts
        group = agg[row] - first_coarse
        inside = (group >= 0) & (group < COARSE)
        fine = inside & (refine[row] == 1)
        for k in range(SLOTS):
            live = inside if k < LIVE else fine
            column = cols[row, k] - first_row
            seg = group * SLOTS + target[row, k]
            here = (column >= 0) & (column < ROWS)
            slot = row * SLOTS + k
            entry = slot + seg * 4096
            place = jnp.where(column < 0, column + ROWS, column)
            own[own_n] = entry + (column & 15) * 128
            halo[halo_n] = entry + (place & 31) * 128
            own_n += (live & here).astype(jnp.int32)
            halo_n += (live & jnp.logical_not(here)).astype(jnp.int32)
        return own_n, halo_n

    own_n, halo_n = lax.fori_loop(0, ROWS, listing, (0, 0))
    for j in range(UNROLL):
        own[own_n + j] = DUMP * 4096
        halo[halo_n + j] = DUMP * 4096
    halo_count[0] = halo_n

    def multiply(row, carry):
        turned = p[row].T
        for k in range(LIVE):
            left[row * SLOTS + k] = dot(turned, a[row, k]).astype(BF16)

        @pl.when(refine[row] == 1)
        def _():
            for k in range(LIVE, SLOTS):
                left[row * SLOTS + k] = dot(turned, a[row, k]).astype(BF16)

        return carry

    lax.fori_loop(0, ROWS, multiply, 0)
    acc[...] = jnp.zeros(acc.shape, F32)
    add_items(own_n, own, left, p, acc, True)

    def keep(at, carry):
        for j in range(UNROLL):
            n = at * UNROLL + j
            left_halo[n] = left[halo[n] & 127]
        return carry

    lax.fori_loop(0, (halo_n + UNROLL - 1) // UNROLL, keep, 0)


def halo_kernel(cols, halo, halo_count, acc_in, left_halo, from_a, from_b, acc, table, sems):
    odd = (cols[0, 0] // ROWS) % 2
    copies = [
        pltpu.make_async_copy(from_a, table.at[pl.ds(odd * ROWS, ROWS)], sems.at[0]),
        pltpu.make_async_copy(from_b, table.at[pl.ds((1 - odd) * ROWS, ROWS)], sems.at[1]),
    ]
    for copy in copies:
        copy.start()
    acc[...] = acc_in[...]
    for copy in copies:
        copy.wait()
    add_items(halo_count[0], halo, left_halo, table, acc, False)


def last_kernel(cols, acc, msg_a, msg_b, p, from_a, from_b, before, after, out, table, rest, sems):
    odd = (cols[0, 0] // ROWS) % 2
    copies = [
        pltpu.make_async_copy(before, table.at[pl.ds(0, 2)], sems.at[0]),
        pltpu.make_async_copy(from_a, table.at[pl.ds(2 + odd * 2 * ROWS, ROWS)], sems.at[1]),
        pltpu.make_async_copy(p, table.at[pl.ds(2 + ROWS, ROWS)], sems.at[2]),
        pltpu.make_async_copy(from_b, table.at[pl.ds(2 + (1 - odd) * 2 * ROWS, ROWS)], sems.at[3]),
        pltpu.make_async_copy(after, table.at[pl.ds(2 + 3 * ROWS, 2)], sems.at[4]),
    ]
    for copy in copies:
        copy.start()
    lane = lax.broadcasted_iota(jnp.int32, (1, DIM), 1)
    scale = jnp.where(lane % 2 == 0, 1.0, 64.0)
    codes = []
    for msg in (msg_a, msg_b):
        note = msg[SLOTS * DIM : MSG, :].astype(F32)[0:1] * scale
        for k in range(SLOTS):
            codes.append(jnp.sum(jnp.where(lane // 2 == k, note, 0.0)).astype(jnp.int32))
    for copy in copies:
        copy.wait()
    rest[...] = jnp.zeros(rest.shape, F32)
    for side, msg in enumerate((msg_a, msg_b)):
        above = odd if side == 0 else 1 - odd
        parts = []
        for k in range(SLOTS):
            code = codes[side * SLOTS + k]
            aim = code >> 6
            seg = above * (SLOTS + 1) + aim
            parts.append((seg, dot(msg[k * DIM : (k + 1) * DIM, :], table[code & 63])))
        for seg, part in parts:
            rest[seg] += part
    for s in range(SEGS):
        value = acc[s]
        if s < SLOTS:
            value = value + rest[s]
        if s >= SEGS - SLOTS:
            value = value + rest[SLOTS + 1 + s - (SEGS - SLOTS)]
        out[s // SLOTS, s % SLOTS] = value.astype(BF16)


def call(kernel, ins, outs, out_specs, in_specs, scratch, cost, **more):
    return pl.pallas_call(
        kernel,
        out_shape=outs,
        in_specs=in_specs,
        out_specs=out_specs,
        scratch_shapes=scratch,
        cost_estimate=pl.CostEstimate(flops=cost[0], bytes_accessed=cost[1], transcendentals=0),
        compiler_params=pltpu.CompilerParams(vmem_limit_bytes=40 * 1024 * 1024),
        **more,
    )(*ins)


def body(a_blocks, p_blocks, a_cols, a_target, agg, refine):
    count = lax.axis_size(AXES)
    shape = jax.ShapeDtypeStruct
    odd_pairs = [(i, i + 1) for i in range(1, count - 1, 2)]
    even_pairs = [(i, i + 1) for i in range(0, count, 2)]
    pairs_a = odd_pairs + [(j, i) for i, j in odd_pairs]
    pairs_b = even_pairs + [(j, i) for i, j in even_pairs]
    two_up = [(i, i + 2) for i in range(count - 2)]
    two_down = [(j, i) for i, j in two_up]
    block_cost = 2 * DIM**3

    from_a = lax.ppermute(p_blocks, AXES, pairs_a)
    from_b = lax.ppermute(p_blocks, AXES, pairs_b)
    ints = (a_cols, a_target, agg, refine)
    msg_a, msg_b = call(
        edge_kernel,
        (*ints, a_blocks, p_blocks),
        [shape((MSG, DIM), BF16)] * 2,
        [VMEM] * 2,
        [SMEM] * 4 + [ANY] * 2,
        [
            pltpu.VMEM((2, SLOTS, DIM, DIM), BF16),
            pltpu.VMEM((2, DIM, DIM), BF16),
            pltpu.SemaphoreType.DMA((4,)),
        ],
        (14 * block_cost, 28 * 32768),
    )
    got_a = lax.ppermute(msg_a, AXES, pairs_a)
    got_b = lax.ppermute(msg_b, AXES, pairs_b)
    before = lax.ppermute(p_blocks[ROWS - 2 :], AXES, two_up)
    after = lax.ppermute(p_blocks[:2], AXES, two_down)
    acc, left_halo, halo, halo_count = call(
        own_kernel,
        (*ints, a_blocks, p_blocks),
        [
            shape((SEGS + 1, DIM, DIM), F32),
            shape((HALO_MAX, DIM, DIM), BF16),
            shape((LIST,), jnp.int32),
            shape((1,), jnp.int32),
        ],
        [VMEM, VMEM, SMEM, SMEM],
        [SMEM] * 4 + [VMEM] * 2,
        [pltpu.SMEM((LIST,), jnp.int32), pltpu.VMEM((ROWS * SLOTS, DIM, DIM), BF16)],
        (128 * block_cost, 8 << 20),
    )
    acc = call(
        halo_kernel,
        (a_cols, halo, halo_count, acc, left_halo, from_a, from_b),
        shape((SEGS + 1, DIM, DIM), F32),
        VMEM,
        [SMEM] * 3 + [VMEM] * 2 + [ANY] * 2,
        [pltpu.VMEM((2 * ROWS, DIM, DIM), BF16), pltpu.SemaphoreType.DMA((2,))],
        (32 * block_cost, 6 << 20),
    )
    return call(
        last_kernel,
        (a_cols, acc, got_a, got_b, p_blocks, from_a, from_b, before, after),
        shape((COARSE, SLOTS, DIM, DIM), BF16),
        VMEM,
        [SMEM] + [VMEM] * 3 + [ANY] * 5,
        [
            pltpu.VMEM((3 * ROWS + 4, DIM, DIM), BF16),
            pltpu.VMEM((2 * (SLOTS + 1), DIM, DIM), F32),
            pltpu.SemaphoreType.DMA((5,)),
        ],
        (14 * block_cost, 5 << 20),
    )


def solution(mesh):
    return jax.shard_map(
        body,
        mesh=mesh,
        in_specs=(
            P(AXES, None, None, None),
            P(AXES, None, None),
            P(AXES, None),
            P(AXES, None),
            P(AXES),
            P(AXES),
        ),
        out_specs=P(AXES, None, None, None),
        check_vma=False,
    )
```

```python
import jax
import jax.numpy as jnp
from jax import lax
from jax.experimental import pallas as pl
from jax.experimental.pallas import tpu as pltpu
from jax.sharding import PartitionSpec as P

ROWS = 16
DIM = 128
SLOTS = 7
LIVE = 3
COARSE = 4
SEGS = COARSE * SLOTS
UNROLL = 8
HALO_MAX = 64 + UNROLL
EDGE_MAX = 16 + UNROLL
LIST = 128
AXES = ("dom", "sub")
F32 = jnp.float32
BF16 = jnp.bfloat16

SMEM = pl.BlockSpec(memory_space=pltpu.SMEM)
VMEM = pl.BlockSpec(memory_space=pltpu.VMEM)
SHAPE = jax.ShapeDtypeStruct
BLOCK_COST = 2 * DIM**3


def dot(x, y):
    return jnp.dot(x, y, preferred_element_type=F32)


def add_items(count, codes, left, right, acc, by_slot):
    def step(at, carry):
        parts = []
        for j in range(UNROLL):
            n = at * UNROLL + j
            code = codes[n]
            slot = (code & 127) if by_slot else n
            parts.append((code >> 12, dot(left[slot], right((code >> 7) & 31))))
        for seg, part in parts:
            acc[seg] += part
        return carry

    lax.fori_loop(0, (count + UNROLL - 1) // UNROLL, step, 0)


def list_kernel(ints, own, halo, edge, counts):
    first_row = ints[0, 0]
    first_coarse = first_row // COARSE

    def listing(row, found):
        own_n, halo_n, edge_n = found
        group = ints[2 * SLOTS, row] - first_coarse
        inside = (group >= 0) & (group < COARSE)
        fine = ints[2 * SLOTS + 1, row] == 1
        for k in range(SLOTS):
            live = True if k < LIVE else fine
            column = ints[k, row] - first_row
            aim = ints[SLOTS + k, row]
            here = (column >= 0) & (column < ROWS)
            place = (jnp.where(column < 0, column + ROWS, column) & 31) * 128
            side = jnp.where(group < 0, 0, SLOTS) + aim
            home = group * SLOTS + aim
            slot = row * SLOTS + k
            own[own_n] = slot + place + jnp.where(inside, home, SEGS + 1 + side) * 4096
            halo[halo_n] = slot + place + home * 4096
            edge[edge_n] = slot + place + side * 4096
            away = live & jnp.logical_not(here)
            own_n += (live & here).astype(jnp.int32)
            halo_n += (away & inside).astype(jnp.int32)
            edge_n += (away & jnp.logical_not(inside)).astype(jnp.int32)
        return own_n, halo_n, edge_n

    own_n, halo_n, edge_n = lax.fori_loop(0, ROWS, listing, (0, 0, 0))
    for j in range(UNROLL):
        own[own_n + j] = SEGS * 4096
        halo[halo_n + j] = SEGS * 4096
        edge[edge_n + j] = 2 * SLOTS * 4096
    counts[0] = halo_n
    counts[1] = edge_n
    counts[2] = (first_row // ROWS) % 2
    counts[3] = own_n


def own_kernel(own, halo, edge, counts, a, p, acc, edge_acc, left_halo, left_edge, left, total):
    total[...] = jnp.zeros(total.shape, F32)
    for row in range(ROWS):
        turned = p[row].T
        for k in range(0, SLOTS, 2):
            if k + 1 < SLOTS:
                both = dot(turned, jnp.concatenate([a[row, k], a[row, k + 1]], axis=1)).astype(BF16)
                left[row * SLOTS + k] = both[:, :DIM]
                left[row * SLOTS + k + 1] = both[:, DIM:]
            else:
                left[row * SLOTS + k] = dot(turned, a[row, k]).astype(BF16)
    add_items(counts[3], own, left, lambda at: p[at & 15], total, True)
    acc[...] = total[: SEGS + 1]
    edge_acc[...] = total[SEGS + 1 :]

    def keep_in(codes, kept):
        def keep(at, carry):
            for j in range(UNROLL):
                n = at * UNROLL + j
                kept[n] = left[codes[n] & 127]
            return carry

        return keep

    lax.fori_loop(0, (counts[0] + UNROLL - 1) // UNROLL, keep_in(halo, left_halo), 0)
    lax.fori_loop(0, (counts[1] + UNROLL - 1) // UNROLL, keep_in(edge, left_edge), 0)


def picker(odd, from_a, from_b):
    return lambda at: jnp.where((at >> 4) == odd, from_a[at & 15], from_b[at & 15])


def edge_kernel(edge, counts, edge_acc, left_edge, from_a, from_b, msg_a, msg_b, total):
    odd = counts[2]
    total[...] = edge_acc[...]
    add_items(counts[1], edge, left_edge, picker(odd, from_a, from_b), total, False)
    for s in range(SLOTS):
        msg_a[s] = total[odd * SLOTS + s].astype(BF16)
        msg_b[s] = total[(1 - odd) * SLOTS + s].astype(BF16)


def halo_kernel(halo, counts, acc_in, left_halo, from_a, from_b, acc):
    acc[...] = acc_in[...]
    add_items(counts[0], halo, left_halo, picker(counts[2], from_a, from_b), acc, False)


def last_kernel(counts, acc, got_a, got_b, out):
    odd = counts[2] == 1
    for s in range(SEGS):
        value = acc[s]
        if s < SLOTS:
            value = value + jnp.where(odd, got_b[s], got_a[s]).astype(F32)
        if s >= SEGS - SLOTS:
            at = s - (SEGS - SLOTS)
            value = value + jnp.where(odd, got_a[at], got_b[at]).astype(F32)
        out[s // SLOTS, s % SLOTS] = value.astype(BF16)


def call(kernel, ins, smems, outs, out_specs, scratch, blocks, size):
    return pl.pallas_call(
        kernel,
        out_shape=outs,
        in_specs=[SMEM] * smems + [VMEM] * (len(ins) - smems),
        out_specs=out_specs,
        scratch_shapes=scratch,
        cost_estimate=pl.CostEstimate(flops=blocks * BLOCK_COST, bytes_accessed=size, transcendentals=0),
        compiler_params=pltpu.CompilerParams(vmem_limit_bytes=36 * 1024 * 1024),
    )(*ins)


def list_part(ints):
    return call(
        list_kernel,
        (ints,),
        1,
        [SHAPE((LIST,), jnp.int32)] * 3 + [SHAPE((4,), jnp.int32)],
        [SMEM] * 4,
        [],
        256,
        1 << 20,
    )


def own_part(own, halo, edge, counts, a_blocks, p_blocks):
    return call(
        own_kernel,
        (own, halo, edge, counts, a_blocks, p_blocks),
        4,
        [
            SHAPE((SEGS + 1, DIM, DIM), F32),
            SHAPE((2 * SLOTS + 1, DIM, DIM), F32),
            SHAPE((HALO_MAX, DIM, DIM), BF16),
            SHAPE((EDGE_MAX, DIM, DIM), BF16),
        ],
        [VMEM] * 4,
        [
            pltpu.VMEM((ROWS * SLOTS, DIM, DIM), BF16),
            pltpu.VMEM((SEGS + 2 * SLOTS + 2, DIM, DIM), F32),
        ],
        128,
        8 << 20,
    )


def edge_part(edge, counts, edge_acc, left_edge, from_a, from_b):
    return call(
        edge_kernel,
        (edge, counts, edge_acc, left_edge, from_a, from_b),
        2,
        [SHAPE((SLOTS, DIM, DIM), BF16)] * 2,
        [VMEM] * 2,
        [pltpu.VMEM((2 * SLOTS + 1, DIM, DIM), F32)],
        8,
        2 << 20,
    )


def halo_part(halo, counts, acc, left_halo, from_a, from_b):
    return call(
        halo_kernel,
        (halo, counts, acc, left_halo, from_a, from_b),
        2,
        SHAPE((SEGS + 1, DIM, DIM), F32),
        VMEM,
        [],
        32,
        6 << 20,
    )


def last_part(counts, acc, got_a, got_b):
    return call(
        last_kernel,
        (counts, acc, got_a, got_b),
        1,
        SHAPE((COARSE, SLOTS, DIM, DIM), BF16),
        VMEM,
        [],
        1,
        4 << 20,
    )


def body(a_blocks, p_blocks, a_cols, a_target, agg, refine):
    count = lax.axis_size(AXES)
    odd_pairs = [(i, i + 1) for i in range(1, count - 1, 2)]
    even_pairs = [(i, i + 1) for i in range(0, count, 2)]
    pairs_a = odd_pairs + [(j, i) for i, j in odd_pairs]
    pairs_b = even_pairs + [(j, i) for i, j in even_pairs]
    ints = jnp.concatenate([a_cols.T, a_target.T, agg[None], refine[None]])

    from_a = lax.ppermute(p_blocks, AXES, pairs_a)
    from_b = lax.ppermute(p_blocks, AXES, pairs_b)
    own, halo, edge, counts = list_part(ints)
    acc, edge_acc, left_halo, left_edge = own_part(own, halo, edge, counts, a_blocks, p_blocks)
    msg_a, msg_b = edge_part(edge, counts, edge_acc, left_edge, from_a, from_b)
    got_a = lax.ppermute(msg_a, AXES, pairs_a)
    got_b = lax.ppermute(msg_b, AXES, pairs_b)
    acc = halo_part(halo, counts, acc, left_halo, from_a, from_b)
    return last_part(counts, acc, got_a, got_b)


def solution(mesh):
    return jax.shard_map(
        body,
        mesh=mesh,
        in_specs=(
            P(AXES, None, None, None),
            P(AXES, None, None),
            P(AXES, None),
            P(AXES, None),
            P(AXES),
            P(AXES),
        ),
        out_specs=P(AXES, None, None, None),
        check_vma=False,
    )
```

```python
import jax
import jax.numpy as jnp
from jax import lax
from jax.experimental import pallas as pl
from jax.experimental.pallas import tpu as pltpu
from jax.sharding import PartitionSpec as P

ROWS = 16
DIM = 128
SLOTS = 7
LIVE = 3
COARSE = 4
SEGS = COARSE * SLOTS
UNROLL = 8
HALO_MAX = 64 + UNROLL
EDGE_MAX = 16 + UNROLL
LIST = 128
OWN, HALO, EDGE, COUNTS = 0, LIST, 2 * LIST, 3 * LIST
AXES = ("dom", "sub")
F32 = jnp.float32
BF16 = jnp.bfloat16

SMEM = pl.BlockSpec(memory_space=pltpu.SMEM)
VMEM = pl.BlockSpec(memory_space=pltpu.VMEM)
ANY = pl.BlockSpec(memory_space=pl.ANY)
SHAPE = jax.ShapeDtypeStruct
BLOCK_COST = 2 * DIM**3


def color_of(edge):
    return 2 if edge % 128 == 126 else edge % 2


def color_in_kernel(edge):
    return jnp.where((edge & 127) == 126, 2, edge & 1)


def dot(x, y):
    return jnp.dot(x, y, preferred_element_type=F32)


def add_items(count, table, base, left, right, acc, by_slot):
    def step(at, carry):
        parts = []
        for j in range(UNROLL):
            n = at * UNROLL + j
            code = table[base + n]
            slot = (code & 127) if by_slot else n
            parts.append((code >> 12, dot(left[slot], right((code >> 7) & 31))))
        for seg, part in parts:
            acc[seg] += part
        return carry

    lax.fori_loop(0, (count + UNROLL - 1) // UNROLL, step, 0)


def list_kernel(ints, table):
    first_row = ints[0, 0]
    first_coarse = first_row // COARSE

    def listing(row, found):
        own_n, halo_n, edge_n = found
        group = ints[2 * SLOTS, row] - first_coarse
        inside = (group >= 0) & (group < COARSE)
        fine = ints[2 * SLOTS + 1, row] == 1
        for k in range(SLOTS):
            live = True if k < LIVE else fine
            column = ints[k, row] - first_row
            aim = ints[SLOTS + k, row]
            here = (column >= 0) & (column < ROWS)
            place = (jnp.where(column < 0, column + ROWS, column) & 31) * 128
            side = jnp.where(group < 0, 0, SLOTS) + aim
            home = group * SLOTS + aim
            slot = row * SLOTS + k
            table[OWN + own_n] = slot + place + jnp.where(inside, home, SEGS + 1 + side) * 4096
            table[HALO + halo_n] = slot + place + home * 4096
            table[EDGE + edge_n] = slot + place + side * 4096
            away = live & jnp.logical_not(here)
            own_n += (live & here).astype(jnp.int32)
            halo_n += (away & inside).astype(jnp.int32)
            edge_n += (away & jnp.logical_not(inside)).astype(jnp.int32)
        return own_n, halo_n, edge_n

    own_n, halo_n, edge_n = lax.fori_loop(0, ROWS, listing, (0, 0, 0))
    for j in range(UNROLL):
        table[OWN + own_n + j] = SEGS * 4096
        table[HALO + halo_n + j] = SEGS * 4096
        table[EDGE + edge_n + j] = 2 * SLOTS * 4096
    table[COUNTS + 0] = halo_n
    table[COUNTS + 1] = edge_n
    table[COUNTS + 2] = own_n
    table[COUNTS + 3] = color_in_kernel(first_row // ROWS - 1)
    table[COUNTS + 4] = color_in_kernel(first_row // ROWS)


def own_kernel(table, a, p, acc, edge_acc, left_halo, left_edge, left, total):
    total[...] = jnp.zeros(total.shape, F32)
    for row in range(ROWS):
        turned = p[row].T
        for k in range(0, SLOTS, 2):
            if k + 1 < SLOTS:
                both = dot(turned, jnp.concatenate([a[row, k], a[row, k + 1]], axis=1)).astype(BF16)
                left[row * SLOTS + k] = both[:, :DIM]
                left[row * SLOTS + k + 1] = both[:, DIM:]
            else:
                left[row * SLOTS + k] = dot(turned, a[row, k]).astype(BF16)
    add_items(table[COUNTS + 2], table, OWN, left, lambda at: p[at & 15], total, True)
    acc[...] = total[: SEGS + 1]
    edge_acc[...] = total[SEGS + 1 :]

    def keep_in(base, kept):
        def keep(at, carry):
            for j in range(UNROLL):
                n = at * UNROLL + j
                kept[n] = left[table[base + n] & 127]
            return carry

        return keep

    lax.fori_loop(0, (table[COUNTS + 0] + UNROLL - 1) // UNROLL, keep_in(HALO, left_halo), 0)
    lax.fori_loop(0, (table[COUNTS + 1] + UNROLL - 1) // UNROLL, keep_in(EDGE, left_edge), 0)


def choose(color, values):
    return jnp.where(color == 0, values[0], jnp.where(color == 1, values[1], values[2]))


def picker(table, sources):
    def right(at):
        color = jnp.where(at < ROWS, table[COUNTS + 3], table[COUNTS + 4])
        return choose(color, [source[at & 15] for source in sources])

    return right


def edge_kernel(table, edge_acc, left_edge, from_0, from_1, from_2, msg_0, msg_1, msg_2, total):
    total[...] = edge_acc[...]
    add_items(table[COUNTS + 1], table, EDGE, left_edge, picker(table, (from_0, from_1, from_2)), total, False)
    for color, msg in enumerate((msg_0, msg_1, msg_2)):
        side = jnp.where(table[COUNTS + 4] == color, SLOTS, 0)
        for s in range(SLOTS):
            msg[s] = total[side + s].astype(BF16)


def halo_kernel(table, acc_in, left_halo, from_0, from_1, from_2, acc, out, total, inner, sem):
    total[...] = acc_in[...]
    add_items(table[COUNTS + 0], table, HALO, left_halo, picker(table, (from_0, from_1, from_2)), total, False)
    for s in range(SLOTS, SEGS - SLOTS):
        inner[s // SLOTS - 1, s % SLOTS] = total[s].astype(BF16)
    copy = pltpu.make_async_copy(inner, out.at[pl.ds(1, COARSE - 2)], sem)
    copy.start()
    acc[:SLOTS] = total[:SLOTS]
    acc[SLOTS:] = total[SEGS - SLOTS : SEGS]
    copy.wait()


def last_kernel(acc, got_0, got_1, got_2, out_in, out, outer, sems):
    got = (got_0, got_1, got_2)
    device = lax.axis_index(AXES[0]) * lax.axis_size(AXES[1]) + lax.axis_index(AXES[1])
    copies = []
    for side, row in enumerate((0, COARSE - 1)):
        color = color_in_kernel(device - 1 + side)
        for s in range(SLOTS):
            value = acc[side * SLOTS + s] + choose(color, [g[s] for g in got]).astype(F32)
            outer[side, s] = value.astype(BF16)
        copies.append(pltpu.make_async_copy(outer.at[side], out.at[row], sems.at[side]))
        copies[-1].start()
    for copy in copies:
        copy.wait()


def call(kernel, ins, smems, outs, out_specs, scratch, blocks, size, anys=0, aliases={}):
    return pl.pallas_call(
        kernel,
        out_shape=outs,
        in_specs=[SMEM] * smems + [VMEM] * (len(ins) - smems - anys) + [ANY] * anys,
        out_specs=out_specs,
        scratch_shapes=scratch,
        input_output_aliases=aliases,
        cost_estimate=pl.CostEstimate(flops=blocks * BLOCK_COST, bytes_accessed=size, transcendentals=0),
        compiler_params=pltpu.CompilerParams(vmem_limit_bytes=36 * 1024 * 1024),
    )(*ins)


def list_part(ints):
    return call(
        list_kernel,
        (ints,),
        1,
        SHAPE((COUNTS + 16,), jnp.int32),
        SMEM,
        [],
        2048,
        1 << 20,
    )


def own_part(table, a_blocks, p_blocks):
    return call(
        own_kernel,
        (table, a_blocks, p_blocks),
        1,
        [
            SHAPE((SEGS + 1, DIM, DIM), F32),
            SHAPE((2 * SLOTS + 1, DIM, DIM), F32),
            SHAPE((HALO_MAX, DIM, DIM), BF16),
            SHAPE((EDGE_MAX, DIM, DIM), BF16),
        ],
        [VMEM] * 4,
        [
            pltpu.VMEM((ROWS * SLOTS, DIM, DIM), BF16),
            pltpu.VMEM((SEGS + 2 * SLOTS + 2, DIM, DIM), F32),
        ],
        128,
        8 << 20,
    )


def edge_part(table, edge_acc, left_edge, sources):
    return call(
        edge_kernel,
        (table, edge_acc, left_edge, *sources),
        1,
        [SHAPE((SLOTS, DIM, DIM), BF16)] * 3,
        [VMEM] * 3,
        [pltpu.VMEM((2 * SLOTS + 1, DIM, DIM), F32)],
        8,
        2 << 20,
    )


def halo_part(table, acc, left_halo, sources):
    return call(
        halo_kernel,
        (table, acc, left_halo, *sources),
        1,
        [SHAPE((2 * SLOTS, DIM, DIM), F32), SHAPE((COARSE, SLOTS, DIM, DIM), BF16)],
        [VMEM, ANY],
        [
            pltpu.VMEM((SEGS + 1, DIM, DIM), F32),
            pltpu.VMEM((COARSE - 2, SLOTS, DIM, DIM), BF16),
            pltpu.SemaphoreType.DMA(()),
        ],
        32,
        6 << 20,
    )


def last_part(acc, got, out):
    return call(
        last_kernel,
        (acc, *got, out),
        0,
        SHAPE((COARSE, SLOTS, DIM, DIM), BF16),
        ANY,
        [pltpu.VMEM((2, SLOTS, DIM, DIM), BF16), pltpu.SemaphoreType.DMA((2,))],
        1,
        2 << 20,
        1,
        {4: 0},
    )


def body(a_blocks, p_blocks, a_cols, a_target, agg, refine):
    count = lax.axis_size(AXES)
    pairs = [[], [], []]
    for i in range(count - 1):
        pairs[color_of(i)] += [(i, i + 1), (i + 1, i)]
    ints = jnp.concatenate([a_cols.T, a_target.T, agg[None], refine[None]])

    from_0 = lax.ppermute(p_blocks, AXES, pairs[0])
    table = list_part(ints)
    from_1 = lax.ppermute(p_blocks, AXES, pairs[1])
    from_2 = lax.ppermute(p_blocks, AXES, pairs[2])
    sources = (from_0, from_1, from_2)
    acc, edge_acc, left_halo, left_edge = own_part(table, a_blocks, p_blocks)
    msg_0, msg_1, msg_2 = edge_part(table, edge_acc, left_edge, sources)
    got = [lax.ppermute(msg, AXES, pairs[color]) for color, msg in ((0, msg_0), (1, msg_1), (2, msg_2))]
    acc, out = halo_part(table, acc, left_halo, sources)
    return last_part(acc, got, out)


def solution(mesh):
    return jax.shard_map(
        body,
        mesh=mesh,
        in_specs=(
            P(AXES, None, None, None),
            P(AXES, None, None),
            P(AXES, None),
            P(AXES, None),
            P(AXES),
            P(AXES),
        ),
        out_specs=P(AXES, None, None, None),
        check_vma=False,
    )
```

```python
import jax
import jax.numpy as jnp
from jax import lax
from jax.experimental import pallas as pl
from jax.experimental.pallas import tpu as pltpu
from jax.sharding import PartitionSpec as P

ROWS = 16
DIM = 128
SLOTS = 7
LIVE = 3
COARSE = 4
SEGS = COARSE * SLOTS
UNROLL = 8
HALO_MAX = 64 + UNROLL
EDGE_MAX = 16 + UNROLL
LIST = 128
OWN, HALO, EDGE, COUNTS = 0, LIST, 2 * LIST, 3 * LIST
AXES = ("dom", "sub")
F32 = jnp.float32
BF16 = jnp.bfloat16

SMEM = pl.BlockSpec(memory_space=pltpu.SMEM)
VMEM = pl.BlockSpec(memory_space=pltpu.VMEM)
ANY = pl.BlockSpec(memory_space=pl.ANY)
SHAPE = jax.ShapeDtypeStruct
BLOCK_COST = 2 * DIM**3


def color_of(edge):
    return 2 if edge % 128 == 126 else edge % 2


def color_in_kernel(edge):
    return jnp.where((edge & 127) == 126, 2, edge & 1)


def dot(x, y):
    return jnp.dot(x, y, preferred_element_type=F32)


def add_items(count, table, base, left, right, acc, by_slot):
    def step(at, carry):
        parts = []
        for j in range(UNROLL):
            n = at * UNROLL + j
            code = table[base + n]
            slot = (code & 127) if by_slot else n
            parts.append((code >> 12, dot(left[slot], right((code >> 7) & 31))))
        for seg, part in parts:
            acc[seg] += part
        return carry

    lax.fori_loop(0, (count + UNROLL - 1) // UNROLL, step, 0)


def list_kernel(ints, table):
    first_row = ints[0, 0]
    first_coarse = first_row // COARSE

    def listing(row, found):
        own_n, halo_n, edge_n = found
        group = ints[2 * SLOTS, row] - first_coarse
        inside = (group >= 0) & (group < COARSE)
        fine = ints[2 * SLOTS + 1, row] == 1
        for k in range(SLOTS):
            live = True if k < LIVE else fine
            column = ints[k, row] - first_row
            aim = ints[SLOTS + k, row]
            here = (column >= 0) & (column < ROWS)
            place = (jnp.where(column < 0, column + ROWS, column) & 31) * 128
            side = jnp.where(group < 0, 0, SLOTS) + aim
            home = group * SLOTS + aim
            slot = row * SLOTS + k
            table[OWN + own_n] = slot + place + jnp.where(inside, home, SEGS + 1 + side) * 4096
            table[HALO + halo_n] = slot + place + home * 4096
            table[EDGE + edge_n] = slot + place + side * 4096
            away = live & jnp.logical_not(here)
            own_n += (live & here).astype(jnp.int32)
            halo_n += (away & inside).astype(jnp.int32)
            edge_n += (away & jnp.logical_not(inside)).astype(jnp.int32)
        return own_n, halo_n, edge_n

    own_n, halo_n, edge_n = lax.fori_loop(0, ROWS, listing, (0, 0, 0))
    for j in range(UNROLL):
        table[OWN + own_n + j] = SEGS * 4096
        table[HALO + halo_n + j] = SEGS * 4096
        table[EDGE + edge_n + j] = 2 * SLOTS * 4096
    table[COUNTS + 0] = halo_n
    table[COUNTS + 1] = edge_n
    table[COUNTS + 2] = own_n
    table[COUNTS + 3] = color_in_kernel(first_row // ROWS - 1)
    table[COUNTS + 4] = color_in_kernel(first_row // ROWS)


def own_kernel(table, a, p, acc, edge_acc, left_halo, left_edge, left, total):
    total[...] = jnp.zeros(total.shape, F32)
    for row in range(ROWS):
        turned = p[row].T
        for k in range(0, SLOTS, 2):
            if k + 1 < SLOTS:
                both = dot(turned, jnp.concatenate([a[row, k], a[row, k + 1]], axis=1)).astype(BF16)
                left[row * SLOTS + k] = both[:, :DIM]
                left[row * SLOTS + k + 1] = both[:, DIM:]
            else:
                left[row * SLOTS + k] = dot(turned, a[row, k]).astype(BF16)
    add_items(table[COUNTS + 2], table, OWN, left, lambda at: p[at & 15], total, True)
    acc[...] = total[: SEGS + 1]
    edge_acc[...] = total[SEGS + 1 :]

    def keep_in(base, kept):
        def keep(at, carry):
            for j in range(UNROLL):
                n = at * UNROLL + j
                kept[n] = left[table[base + n] & 127]
            return carry

        return keep

    lax.fori_loop(0, (table[COUNTS + 0] + UNROLL - 1) // UNROLL, keep_in(HALO, left_halo), 0)
    lax.fori_loop(0, (table[COUNTS + 1] + UNROLL - 1) // UNROLL, keep_in(EDGE, left_edge), 0)


def choose(color, values):
    return jnp.where(color == 0, values[0], jnp.where(color == 1, values[1], values[2]))


def picker(table, sources):
    def right(at):
        color = jnp.where(at < ROWS, table[COUNTS + 3], table[COUNTS + 4])
        return choose(color, [source[at & 15] for source in sources])

    return right


def edge_kernel(table, edge_acc, left_edge, from_0, from_1, from_2, msg_up, msg_down, total):
    total[...] = edge_acc[...]
    add_items(table[COUNTS + 1], table, EDGE, left_edge, picker(table, (from_0, from_1, from_2)), total, False)
    for s in range(SLOTS):
        msg_down[s] = total[s].astype(BF16)
        msg_up[s] = total[SLOTS + s].astype(BF16)


def halo_kernel(table, acc_in, left_halo, from_0, from_1, from_2, acc, out, total, inner, sem):
    total[...] = acc_in[...]
    add_items(table[COUNTS + 0], table, HALO, left_halo, picker(table, (from_0, from_1, from_2)), total, False)
    for s in range(SLOTS, SEGS - SLOTS):
        inner[s // SLOTS - 1, s % SLOTS] = total[s].astype(BF16)
    copy = pltpu.make_async_copy(inner, out.at[pl.ds(1, COARSE - 2)], sem)
    copy.start()
    acc[:SLOTS] = total[:SLOTS]
    acc[SLOTS:] = total[SEGS - SLOTS : SEGS]
    copy.wait()


def last_kernel(acc, from_before, from_after, out_in, out, outer, sems):
    copies = []
    for side, (row, got) in enumerate(((0, from_before), (COARSE - 1, from_after))):
        for s in range(SLOTS):
            outer[side, s] = (acc[side * SLOTS + s] + got[s].astype(F32)).astype(BF16)
        copies.append(pltpu.make_async_copy(outer.at[side], out.at[row], sems.at[side]))
        copies[-1].start()
    for copy in copies:
        copy.wait()


def call(kernel, ins, smems, outs, out_specs, scratch, blocks, size, anys=0, aliases={}):
    return pl.pallas_call(
        kernel,
        out_shape=outs,
        in_specs=[SMEM] * smems + [VMEM] * (len(ins) - smems - anys) + [ANY] * anys,
        out_specs=out_specs,
        scratch_shapes=scratch,
        input_output_aliases=aliases,
        cost_estimate=pl.CostEstimate(flops=blocks * BLOCK_COST, bytes_accessed=size, transcendentals=0),
        compiler_params=pltpu.CompilerParams(vmem_limit_bytes=36 * 1024 * 1024),
    )(*ins)


def list_part(ints):
    return call(
        list_kernel,
        (ints,),
        1,
        SHAPE((COUNTS + 16,), jnp.int32),
        SMEM,
        [],
        2048,
        1 << 20,
    )


def own_part(table, a_blocks, p_blocks):
    return call(
        own_kernel,
        (table, a_blocks, p_blocks),
        1,
        [
            SHAPE((SEGS + 1, DIM, DIM), F32),
            SHAPE((2 * SLOTS + 1, DIM, DIM), F32),
            SHAPE((HALO_MAX, DIM, DIM), BF16),
            SHAPE((EDGE_MAX, DIM, DIM), BF16),
        ],
        [VMEM] * 4,
        [
            pltpu.VMEM((ROWS * SLOTS, DIM, DIM), BF16),
            pltpu.VMEM((SEGS + 2 * SLOTS + 2, DIM, DIM), F32),
        ],
        128,
        8 << 20,
    )


def edge_part(table, edge_acc, left_edge, sources):
    return call(
        edge_kernel,
        (table, edge_acc, left_edge, *sources),
        1,
        [SHAPE((SLOTS, DIM, DIM), BF16)] * 2,
        [VMEM] * 2,
        [pltpu.VMEM((2 * SLOTS + 1, DIM, DIM), F32)],
        8,
        2 << 20,
    )


def halo_part(table, acc, left_halo, sources):
    return call(
        halo_kernel,
        (table, acc, left_halo, *sources),
        1,
        [SHAPE((2 * SLOTS, DIM, DIM), F32), SHAPE((COARSE, SLOTS, DIM, DIM), BF16)],
        [VMEM, ANY],
        [
            pltpu.VMEM((SEGS + 1, DIM, DIM), F32),
            pltpu.VMEM((COARSE - 2, SLOTS, DIM, DIM), BF16),
            pltpu.SemaphoreType.DMA(()),
        ],
        32,
        6 << 20,
    )


def last_part(acc, got, out):
    return call(
        last_kernel,
        (acc, *got, out),
        0,
        SHAPE((COARSE, SLOTS, DIM, DIM), BF16),
        ANY,
        [pltpu.VMEM((2, SLOTS, DIM, DIM), BF16), pltpu.SemaphoreType.DMA((2,))],
        1,
        2 << 20,
        1,
        {3: 0},
    )


def body(a_blocks, p_blocks, a_cols, a_target, agg, refine):
    count = lax.axis_size(AXES)
    pairs = [[], [], []]
    for i in range(count - 1):
        pairs[color_of(i)] += [(i, i + 1), (i + 1, i)]
    ints = jnp.concatenate([a_cols.T, a_target.T, agg[None], refine[None]])

    from_0 = lax.ppermute(p_blocks, AXES, pairs[0])
    table = list_part(ints)
    from_1 = lax.ppermute(p_blocks, AXES, pairs[1])
    from_2 = lax.ppermute(p_blocks, AXES, pairs[2])
    sources = (from_0, from_1, from_2)
    acc, edge_acc, left_halo, left_edge = own_part(table, a_blocks, p_blocks)
    msg_up, msg_down = edge_part(table, edge_acc, left_edge, sources)
    up = [(i, i + 1) for i in range(count - 1)]
    down = [(j, i) for i, j in up]
    got = [lax.ppermute(msg_up, AXES, up), lax.ppermute(msg_down, AXES, down)]
    acc, out = halo_part(table, acc, left_halo, sources)
    return last_part(acc, got, out)


def solution(mesh):
    return jax.shard_map(
        body,
        mesh=mesh,
        in_specs=(
            P(AXES, None, None, None),
            P(AXES, None, None),
            P(AXES, None),
            P(AXES, None),
            P(AXES),
            P(AXES),
        ),
        out_specs=P(AXES, None, None, None),
        check_vma=False,
    )
```

```python
import jax
import jax.numpy as jnp
from jax import lax
from jax.experimental import pallas as pl
from jax.experimental.pallas import tpu as pltpu
from jax.sharding import PartitionSpec as P

ROWS = 16
DIM = 128
SLOTS = 7
LIVE = 3
COARSE = 4
SEGS = COARSE * SLOTS
UNROLL = 8
HALO_MAX = 64 + UNROLL
EDGE_MAX = 16 + UNROLL
LIST = 128
OWN, HALO, EDGE, COUNTS = 0, LIST, 2 * LIST, 3 * LIST
AXES = ("dom", "sub")
F32 = jnp.float32
BF16 = jnp.bfloat16

SMEM = pl.BlockSpec(memory_space=pltpu.SMEM)
VMEM = pl.BlockSpec(memory_space=pltpu.VMEM)
ANY = pl.BlockSpec(memory_space=pl.ANY)
SHAPE = jax.ShapeDtypeStruct
BLOCK_COST = 2 * DIM**3


def color_of(edge):
    return 2 if edge % 128 in (119, 126) else edge % 2


def color_in_kernel(edge):
    return jnp.where(((edge & 127) == 126) | ((edge & 127) == 119), 2, edge & 1)


def dot(x, y):
    return jnp.dot(x, y, preferred_element_type=F32)


def add_items(count, table, base, left, right, acc, by_slot, unroll=UNROLL):
    def step(at, carry):
        parts = []
        for j in range(unroll):
            n = at * unroll + j
            code = table[base + n]
            slot = (code & 127) if by_slot else n
            parts.append((code >> 12, dot(left[slot], right((code >> 7) & 31))))
        for seg, part in parts:
            acc[seg] += part
        return carry

    lax.fori_loop(0, (count + unroll - 1) // unroll, step, 0)


def list_kernel(ints, table):
    first_row = ints[0, 0]
    first_coarse = first_row // COARSE

    def listing(row, found):
        own_n, halo_n, edge_n = found
        group = ints[2 * SLOTS, row] - first_coarse
        inside = (group >= 0) & (group < COARSE)
        fine = ints[2 * SLOTS + 1, row] == 1
        for k in range(SLOTS):
            live = True if k < LIVE else fine
            column = ints[k, row] - first_row
            aim = ints[SLOTS + k, row]
            here = (column >= 0) & (column < ROWS)
            place = (jnp.where(column < 0, column + ROWS, column) & 31) * 128
            side = jnp.where(group < 0, 0, SLOTS) + aim
            home = group * SLOTS + aim
            slot = row * SLOTS + k
            table[OWN + own_n] = slot + place + jnp.where(inside, home, SEGS + 1 + side) * 4096
            table[HALO + halo_n] = slot + place + home * 4096
            table[EDGE + edge_n] = slot + place + side * 4096
            away = live & jnp.logical_not(here)
            own_n += (live & here).astype(jnp.int32)
            halo_n += (away & inside).astype(jnp.int32)
            edge_n += (away & jnp.logical_not(inside)).astype(jnp.int32)
        return own_n, halo_n, edge_n

    own_n, halo_n, edge_n = lax.fori_loop(0, ROWS, listing, (0, 0, 0))
    for j in range(UNROLL):
        table[OWN + own_n + j] = SEGS * 4096
        table[HALO + halo_n + j] = SEGS * 4096
        table[EDGE + edge_n + j] = 2 * SLOTS * 4096
    table[COUNTS + 0] = halo_n
    table[COUNTS + 1] = edge_n
    table[COUNTS + 2] = own_n
    table[COUNTS + 3] = color_in_kernel(first_row // ROWS - 1)
    table[COUNTS + 4] = color_in_kernel(first_row // ROWS)


def own_kernel(table, a, p, acc, edge_acc, left_halo, left_edge, left, total):
    total[...] = jnp.zeros(total.shape, F32)
    for row in range(ROWS):
        turned = p[row].T
        for k in range(0, SLOTS, 2):
            if k + 1 < SLOTS:
                both = dot(turned, jnp.concatenate([a[row, k], a[row, k + 1]], axis=1)).astype(BF16)
                left[row * SLOTS + k] = both[:, :DIM]
                left[row * SLOTS + k + 1] = both[:, DIM:]
            else:
                left[row * SLOTS + k] = dot(turned, a[row, k]).astype(BF16)
    add_items(table[COUNTS + 2], table, OWN, left, lambda at: p[at & 15], total, True)
    acc[...] = total[: SEGS + 1]
    edge_acc[...] = total[SEGS + 1 :]

    def keep_in(base, kept):
        def keep(at, carry):
            for j in range(UNROLL):
                n = at * UNROLL + j
                kept[n] = left[table[base + n] & 127]
            return carry

        return keep

    lax.fori_loop(0, (table[COUNTS + 0] + UNROLL - 1) // UNROLL, keep_in(HALO, left_halo), 0)
    lax.fori_loop(0, (table[COUNTS + 1] + UNROLL - 1) // UNROLL, keep_in(EDGE, left_edge), 0)


def choose(color, values):
    return jnp.where(color == 0, values[0], jnp.where(color == 1, values[1], values[2]))


def picker(table, sources):
    def right(at):
        color = jnp.where(at < ROWS, table[COUNTS + 3], table[COUNTS + 4])
        return choose(color, [source[at & 15] for source in sources])

    return right


def edge_kernel(table, edge_acc, left_edge, from_0, from_1, from_2, msg_up, msg_down, total):
    total[...] = edge_acc[...]
    add_items(table[COUNTS + 1], table, EDGE, left_edge, picker(table, (from_0, from_1, from_2)), total, False, 4)
    for s in range(SLOTS):
        msg_down[s] = total[s].astype(BF16)
        msg_up[s] = total[SLOTS + s].astype(BF16)


def halo_kernel(table, acc_in, left_halo, from_0, from_1, from_2, acc, out, total, inner, sem):
    total[...] = acc_in[...]
    add_items(table[COUNTS + 0], table, HALO, left_halo, picker(table, (from_0, from_1, from_2)), total, False)
    for s in range(SLOTS, SEGS - SLOTS):
        inner[s // SLOTS - 1, s % SLOTS] = total[s].astype(BF16)
    copy = pltpu.make_async_copy(inner, out.at[pl.ds(1, COARSE - 2)], sem)
    copy.start()
    acc[:SLOTS] = total[:SLOTS]
    acc[SLOTS:] = total[SEGS - SLOTS : SEGS]
    copy.wait()


def last_kernel(acc, from_before, from_after, out_in, out, outer, sems):
    copies = []
    for side, (row, got) in enumerate(((0, from_before), (COARSE - 1, from_after))):
        for s in range(SLOTS):
            outer[side, s] = (acc[side * SLOTS + s] + got[s].astype(F32)).astype(BF16)
        copies.append(pltpu.make_async_copy(outer.at[side], out.at[row], sems.at[side]))
        copies[-1].start()
    for copy in copies:
        copy.wait()


def call(kernel, ins, smems, outs, out_specs, scratch, blocks, size, anys=0, aliases={}):
    return pl.pallas_call(
        kernel,
        out_shape=outs,
        in_specs=[SMEM] * smems + [VMEM] * (len(ins) - smems - anys) + [ANY] * anys,
        out_specs=out_specs,
        scratch_shapes=scratch,
        input_output_aliases=aliases,
        cost_estimate=pl.CostEstimate(flops=blocks * BLOCK_COST, bytes_accessed=size, transcendentals=0),
        compiler_params=pltpu.CompilerParams(vmem_limit_bytes=36 * 1024 * 1024),
    )(*ins)


def list_part(ints):
    return call(
        list_kernel,
        (ints,),
        1,
        SHAPE((COUNTS + 16,), jnp.int32),
        SMEM,
        [],
        2048,
        1 << 20,
    )


def own_part(table, a_blocks, p_blocks):
    return call(
        own_kernel,
        (table, a_blocks, p_blocks),
        1,
        [
            SHAPE((SEGS + 1, DIM, DIM), F32),
            SHAPE((2 * SLOTS + 1, DIM, DIM), F32),
            SHAPE((HALO_MAX, DIM, DIM), BF16),
            SHAPE((EDGE_MAX, DIM, DIM), BF16),
        ],
        [VMEM] * 4,
        [
            pltpu.VMEM((ROWS * SLOTS, DIM, DIM), BF16),
            pltpu.VMEM((SEGS + 2 * SLOTS + 2, DIM, DIM), F32),
        ],
        128,
        8 << 20,
    )


def edge_part(table, edge_acc, left_edge, sources):
    return call(
        edge_kernel,
        (table, edge_acc, left_edge, *sources),
        1,
        [SHAPE((SLOTS, DIM, DIM), BF16)] * 2,
        [VMEM] * 2,
        [pltpu.VMEM((2 * SLOTS + 1, DIM, DIM), F32)],
        8,
        2 << 20,
    )


def halo_part(table, acc, left_halo, sources):
    return call(
        halo_kernel,
        (table, acc, left_halo, *sources),
        1,
        [SHAPE((2 * SLOTS, DIM, DIM), F32), SHAPE((COARSE, SLOTS, DIM, DIM), BF16)],
        [VMEM, ANY],
        [
            pltpu.VMEM((SEGS + 1, DIM, DIM), F32),
            pltpu.VMEM((COARSE - 2, SLOTS, DIM, DIM), BF16),
            pltpu.SemaphoreType.DMA(()),
        ],
        32,
        6 << 20,
    )


def last_part(acc, got, out):
    return call(
        last_kernel,
        (acc, *got, out),
        0,
        SHAPE((COARSE, SLOTS, DIM, DIM), BF16),
        ANY,
        [pltpu.VMEM((2, SLOTS, DIM, DIM), BF16), pltpu.SemaphoreType.DMA((2,))],
        1,
        2 << 20,
        1,
        {3: 0},
    )


def body(a_blocks, p_blocks, a_cols, a_target, agg, refine):
    count = lax.axis_size(AXES)
    pairs = [[], [], []]
    for i in range(count - 1):
        pairs[color_of(i)] += [(i, i + 1), (i + 1, i)]
    ints = jnp.concatenate([a_cols.T, a_target.T, agg[None], refine[None]])

    from_0 = lax.ppermute(p_blocks, AXES, pairs[0])
    table = list_part(ints)
    from_1 = lax.ppermute(p_blocks, AXES, pairs[1])
    from_2 = lax.ppermute(p_blocks, AXES, pairs[2])
    sources = (from_0, from_1, from_2)
    acc, edge_acc, left_halo, left_edge = own_part(table, a_blocks, p_blocks)
    msg_up, msg_down = edge_part(table, edge_acc, left_edge, sources)
    up = [(i, i + 1) for i in range(count - 1)]
    down = [(j, i) for i, j in up]
    got = [lax.ppermute(msg_up, AXES, up), lax.ppermute(msg_down, AXES, down)]
    acc, out = halo_part(table, acc, left_halo, sources)
    return last_part(acc, got, out)


def solution(mesh):
    return jax.shard_map(
        body,
        mesh=mesh,
        in_specs=(
            P(AXES, None, None, None),
            P(AXES, None, None),
            P(AXES, None),
            P(AXES, None),
            P(AXES),
            P(AXES),
        ),
        out_specs=P(AXES, None, None, None),
        check_vma=False,
    )
```

```python
import jax
import jax.numpy as jnp
from jax import lax
from jax.experimental import pallas as pl
from jax.experimental.pallas import tpu as pltpu
from jax.sharding import PartitionSpec as P

ROWS = 16
DIM = 128
SLOTS = 7
LIVE = 3
COARSE = 4
SEGS = COARSE * SLOTS
UNROLL = 8
HALO_MAX = 64 + UNROLL
EDGE_MAX = 16 + UNROLL
LIST = 128
OWN, HALO, EDGE, COUNTS = 0, LIST, 2 * LIST, 3 * LIST
AXES = ("dom", "sub")
F32 = jnp.float32
BF16 = jnp.bfloat16

SMEM = pl.BlockSpec(memory_space=pltpu.SMEM)
VMEM = pl.BlockSpec(memory_space=pltpu.VMEM)
ANY = pl.BlockSpec(memory_space=pl.ANY)
SHAPE = jax.ShapeDtypeStruct
BLOCK_COST = 2 * DIM**3


def color_of(edge):
    return 2 if edge % 128 in (64, 119, 126) else edge % 2


def color_in_kernel(edge):
    at = edge & 127
    return jnp.where((at == 64) | (at == 119) | (at == 126), 2, at & 1)


def dot(x, y):
    return jnp.dot(x, y, preferred_element_type=F32)


def add_items(count, table, base, left, right, acc, by_slot, unroll=UNROLL):
    def step(at, carry):
        parts = []
        for j in range(unroll):
            n = at * unroll + j
            code = table[base + n]
            slot = (code & 127) if by_slot else n
            parts.append((code >> 12, dot(left[slot], right((code >> 7) & 31))))
        for seg, part in parts:
            acc[seg] += part
        return carry

    lax.fori_loop(0, (count + unroll - 1) // unroll, step, 0)


def list_kernel(ints, table):
    first_row = ints[0, 0]
    first_coarse = first_row // COARSE

    def listing(row, found):
        own_n, halo_n, edge_n = found
        group = ints[2 * SLOTS, row] - first_coarse
        inside = (group >= 0) & (group < COARSE)
        fine = ints[2 * SLOTS + 1, row] == 1
        for k in range(SLOTS):
            live = True if k < LIVE else fine
            column = ints[k, row] - first_row
            aim = ints[SLOTS + k, row]
            here = (column >= 0) & (column < ROWS)
            place = (jnp.where(column < 0, column + ROWS, column) & 31) * 128
            side = jnp.where(group < 0, 0, SLOTS) + aim
            home = group * SLOTS + aim
            slot = row * SLOTS + k
            table[OWN + own_n] = slot + place + jnp.where(inside, home, SEGS + 1 + side) * 4096
            table[HALO + halo_n] = slot + place + home * 4096
            table[EDGE + edge_n] = slot + place + side * 4096
            away = live & jnp.logical_not(here)
            own_n += (live & here).astype(jnp.int32)
            halo_n += (away & inside).astype(jnp.int32)
            edge_n += (away & jnp.logical_not(inside)).astype(jnp.int32)
        return own_n, halo_n, edge_n

    own_n, halo_n, edge_n = lax.fori_loop(0, ROWS, listing, (0, 0, 0))
    for j in range(UNROLL):
        table[OWN + own_n + j] = SEGS * 4096
        table[HALO + halo_n + j] = SEGS * 4096
        table[EDGE + edge_n + j] = 2 * SLOTS * 4096
    table[COUNTS + 0] = halo_n
    table[COUNTS + 1] = edge_n
    table[COUNTS + 2] = own_n
    table[COUNTS + 3] = color_in_kernel(first_row // ROWS - 1)
    table[COUNTS + 4] = color_in_kernel(first_row // ROWS)


def own_kernel(table, a, p, acc, edge_acc, left_halo, left_edge, left, total):
    total[...] = jnp.zeros(total.shape, F32)
    for row in range(ROWS):
        turned = p[row].T
        for k in range(0, SLOTS, 2):
            if k + 1 < SLOTS:
                both = dot(turned, jnp.concatenate([a[row, k], a[row, k + 1]], axis=1)).astype(BF16)
                left[row * SLOTS + k] = both[:, :DIM]
                left[row * SLOTS + k + 1] = both[:, DIM:]
            else:
                left[row * SLOTS + k] = dot(turned, a[row, k]).astype(BF16)
    add_items(table[COUNTS + 2], table, OWN, left, lambda at: p[at & 15], total, True)
    acc[...] = total[: SEGS + 1]
    edge_acc[...] = total[SEGS + 1 :]

    def keep_in(base, kept):
        def keep(at, carry):
            for j in range(UNROLL):
                n = at * UNROLL + j
                kept[n] = left[table[base + n] & 127]
            return carry

        return keep

    lax.fori_loop(0, (table[COUNTS + 0] + UNROLL - 1) // UNROLL, keep_in(HALO, left_halo), 0)
    lax.fori_loop(0, (table[COUNTS + 1] + UNROLL - 1) // UNROLL, keep_in(EDGE, left_edge), 0)


def choose(color, values):
    return jnp.where(color == 0, values[0], jnp.where(color == 1, values[1], values[2]))


def picker(table, sources):
    def right(at):
        color = jnp.where(at < ROWS, table[COUNTS + 3], table[COUNTS + 4])
        return choose(color, [source[at & 15] for source in sources])

    return right


def edge_kernel(table, edge_acc, left_edge, from_0, from_1, from_2, msg_up, msg_down, total):
    total[...] = edge_acc[...]
    add_items(table[COUNTS + 1], table, EDGE, left_edge, picker(table, (from_0, from_1, from_2)), total, False, 4)
    for s in range(SLOTS):
        msg_down[s] = total[s].astype(BF16)
        msg_up[s] = total[SLOTS + s].astype(BF16)


def halo_kernel(table, acc_in, left_halo, from_0, from_1, from_2, acc, out, total, inner, sem):
    total[...] = acc_in[...]
    add_items(table[COUNTS + 0], table, HALO, left_halo, picker(table, (from_0, from_1, from_2)), total, False)
    for s in range(SLOTS, SEGS - SLOTS):
        inner[s // SLOTS - 1, s % SLOTS] = total[s].astype(BF16)
    copy = pltpu.make_async_copy(inner, out.at[pl.ds(1, COARSE - 2)], sem)
    copy.start()
    acc[:SLOTS] = total[:SLOTS]
    acc[SLOTS:] = total[SEGS - SLOTS : SEGS]
    copy.wait()


def last_kernel(acc, from_before, from_after, out_in, out, outer, sems):
    copies = []
    for side, (row, got) in enumerate(((0, from_before), (COARSE - 1, from_after))):
        for s in range(SLOTS):
            outer[side, s] = (acc[side * SLOTS + s] + got[s].astype(F32)).astype(BF16)
        copies.append(pltpu.make_async_copy(outer.at[side], out.at[row], sems.at[side]))
        copies[-1].start()
    for copy in copies:
        copy.wait()


def call(kernel, ins, smems, outs, out_specs, scratch, blocks, size, anys=0, aliases={}):
    return pl.pallas_call(
        kernel,
        out_shape=outs,
        in_specs=[SMEM] * smems + [VMEM] * (len(ins) - smems - anys) + [ANY] * anys,
        out_specs=out_specs,
        scratch_shapes=scratch,
        input_output_aliases=aliases,
        cost_estimate=pl.CostEstimate(flops=blocks * BLOCK_COST, bytes_accessed=size, transcendentals=0),
        compiler_params=pltpu.CompilerParams(vmem_limit_bytes=36 * 1024 * 1024),
    )(*ins)


def list_part(ints):
    return call(
        list_kernel,
        (ints,),
        1,
        SHAPE((COUNTS + 16,), jnp.int32),
        SMEM,
        [],
        2048,
        1 << 20,
    )


def own_part(table, a_blocks, p_blocks):
    return call(
        own_kernel,
        (table, a_blocks, p_blocks),
        1,
        [
            SHAPE((SEGS + 1, DIM, DIM), F32),
            SHAPE((2 * SLOTS + 1, DIM, DIM), F32),
            SHAPE((HALO_MAX, DIM, DIM), BF16),
            SHAPE((EDGE_MAX, DIM, DIM), BF16),
        ],
        [VMEM] * 4,
        [
            pltpu.VMEM((ROWS * SLOTS, DIM, DIM), BF16),
            pltpu.VMEM((SEGS + 2 * SLOTS + 2, DIM, DIM), F32),
        ],
        128,
        8 << 20,
    )


def edge_part(table, edge_acc, left_edge, sources):
    return call(
        edge_kernel,
        (table, edge_acc, left_edge, *sources),
        1,
        [SHAPE((SLOTS, DIM, DIM), BF16)] * 2,
        [VMEM] * 2,
        [pltpu.VMEM((2 * SLOTS + 1, DIM, DIM), F32)],
        8,
        2 << 20,
    )


def halo_part(table, acc, left_halo, sources):
    return call(
        halo_kernel,
        (table, acc, left_halo, *sources),
        1,
        [SHAPE((2 * SLOTS, DIM, DIM), F32), SHAPE((COARSE, SLOTS, DIM, DIM), BF16)],
        [VMEM, ANY],
        [
            pltpu.VMEM((SEGS + 1, DIM, DIM), F32),
            pltpu.VMEM((COARSE - 2, SLOTS, DIM, DIM), BF16),
            pltpu.SemaphoreType.DMA(()),
        ],
        32,
        6 << 20,
    )


def last_part(acc, got, out):
    return call(
        last_kernel,
        (acc, *got, out),
        0,
        SHAPE((COARSE, SLOTS, DIM, DIM), BF16),
        ANY,
        [pltpu.VMEM((2, SLOTS, DIM, DIM), BF16), pltpu.SemaphoreType.DMA((2,))],
        1,
        2 << 20,
        1,
        {3: 0},
    )


def body(a_blocks, p_blocks, a_cols, a_target, agg, refine):
    count = lax.axis_size(AXES)
    pairs = [[], [], []]
    for i in range(count - 1):
        pairs[color_of(i)] += [(i, i + 1), (i + 1, i)]
    ints = jnp.concatenate([a_cols.T, a_target.T, agg[None], refine[None]])

    from_0 = lax.ppermute(p_blocks, AXES, pairs[0])
    table = list_part(ints)
    from_1 = lax.ppermute(p_blocks, AXES, pairs[1])
    from_2 = lax.ppermute(p_blocks, AXES, pairs[2])
    sources = (from_0, from_1, from_2)
    acc, edge_acc, left_halo, left_edge = own_part(table, a_blocks, p_blocks)
    msg_up, msg_down = edge_part(table, edge_acc, left_edge, sources)
    up = [(i, i + 1) for i in range(count - 1)]
    down = [(j, i) for i, j in up]
    got = [lax.ppermute(msg_up, AXES, up), lax.ppermute(msg_down, AXES, down)]
    acc, out = halo_part(table, acc, left_halo, sources)
    return last_part(acc, got, out)


def solution(mesh):
    return jax.shard_map(
        body,
        mesh=mesh,
        in_specs=(
            P(AXES, None, None, None),
            P(AXES, None, None),
            P(AXES, None),
            P(AXES, None),
            P(AXES),
            P(AXES),
        ),
        out_specs=P(AXES, None, None, None),
        check_vma=False,
    )
```
